256 devices in a mesh: lat: 64 (over x, z, core), lev: 4 (over y).
Axes of the slice: x: 4, y: 4, z: 8, core: 2. Of those that a mesh axis runs over, the one named last changes fastest.
Arguments:
- spectral_in: bfloat16 [16, 640, 2, 1281], P('lev', 'lat'), may hold values from -0.15625 to 0.15625
- legendre: bfloat16 [640, 1280, 1281], P('lat', 'lev'), may hold values from -0.15625 to 0.15625
- weights: float32 [1280], P('lev'), may hold values from 0.5 to 2
- cycle_points: int32 [1280], replicated, may hold values from 12 to 5136, as said below
- assignment: int32 [640], replicated, may hold values from 0 to 639, each once
Outputs:
- spectral_out: float32 [8, 640, 2, 1281], P('lev', 'lat')
The draws below stay inside these ranges and needn't reach their ends.
Inputs may be any that keep to these rules, and one draw needn't show every extreme that they name: cycle_points[j] (j counted from the pole, from 0) is a multiple of 4 from 4 j + 12 to 4 j + 20; the last entry is 5136. `assignment`: every pair number appears once.
All inputs are finite; a program needn't handle non-finite values.
Results may differ from the reference program's by a relative error of at most 0.015.
Values may be sent and summed in bfloat16 or wider, within the bound.
No kernel may reach another device: no remote copies, remote signals or barrier semaphores. Data moves between devices by JAX's collectives and lax.ppermute only.
A program may use at most 128 MiB of HBM per device.

```python
import math
import jax
import jax.numpy as jnp
from jax import lax

NM = 1280
HALF = 1280
FLD = 16
NP = 1281
PAIRS = 640
OUT = 8


def draw_cycle_points(key, part):
    key = jax.random.fold_in(key, 7)
    cycle_index = jnp.arange(HALF, dtype=jnp.int32)
    removed = jax.random.randint(key, (HALF,), 0, 3, dtype=jnp.int32)
    removed = jnp.where(cycle_index == HALF - 1, 0, removed)
    return (4 * cycle_index + 20 - 4 * removed).astype(jnp.int32)


def level_of(stream_key, extent, cuts, smallest, top_value):
    gain, own = 1.0, jax.random.fold_in(stream_key, 6)
    for position, parts in cuts:
        steps = jnp.exp(jax.random.uniform(jax.random.fold_in(own, position), (parts,), jnp.float32, smallest / len(cuts), top_value / len(cuts)))
        gain = gain * jnp.repeat(steps, extent[position] // parts).reshape([-1 if axis == position else 1 for axis in range(len(extent))])
    return gain


def bell_draw(rng, extent, width, most, pieces=(), held_as=jnp.bfloat16):
    values = jax.random.normal(rng, extent, jnp.float32) * width
    if len(pieces) > 0:
        values = level_of(rng, extent, pieces, -0.22, 0.18) * values
    return jnp.clip(values, min=-most, max=most).astype(held_as)


def setup_inputs(seed: int = 0) -> dict:
    arg_keys = jax.random.split(jax.random.key(seed), 6)
    spectral_in = bell_draw(arg_keys[0], (FLD, PAIRS, 2, NP), NM ** -0.5, 0.15625, ((0, 4), (1, 64)))
    legendre = bell_draw(arg_keys[1], (PAIRS, HALF, NP), NM ** -0.5, 0.15625, ((0, 64), (1, 4)))
    weights = jnp.clip(jnp.exp(math.log(2.0) - 1.3862944 * jax.random.uniform(arg_keys[2], (HALF,), jnp.float32) ** level_of(arg_keys[2], (HALF,), ((0, 4),), -0.2, 0.2)), 0.5, 2.0)
    cycle_points = draw_cycle_points(jax.random.fold_in(arg_keys[5], 71), 0)
    assignment = jax.random.permutation(arg_keys[4], NM // 2).astype(jnp.int32)
    return {"spectral_in": spectral_in, "legendre": legendre, "weights": weights, "cycle_points": cycle_points, "assignment": assignment}


def selector_table(pair_ids, total):
    column = jnp.arange(total + 1, dtype=jnp.int32)[None, :]
    split = total - pair_ids[:, None]
    second = (column >= split).astype(jnp.int32)
    parity = jnp.where(second == 1, column - split, column) % 2
    parity_bit = jnp.arange(2, dtype=jnp.int32)[:, None, None, None]
    segment_bit = jnp.arange(2, dtype=jnp.int32)[None, :, None, None]
    chosen = (parity[None, None] == parity_bit) & (second[None, None] == segment_bit)
    return chosen.astype(jnp.bfloat16)

def cycle_transform(coef, lengths, wave_numbers, grid_width):
    row_total = grid_width // 128
    columns = wave_numbers.shape[0]
    row_index = jnp.arange(row_total, dtype=jnp.int32)
    lane_index = jnp.arange(128, dtype=jnp.int32)
    period = lengths[:, None, None]
    turn_rows = wave_numbers[None, None, :] * (128 * row_index)[None, :, None] % period
    turn_lanes = wave_numbers[None, :, None] * lane_index[None, None, :] % period
    step_angle = 2.0 * math.pi / lengths.astype(jnp.float32)
    angle_rows = turn_rows.astype(jnp.float32) * step_angle[:, None, None]
    angle_lanes = turn_lanes.astype(jnp.float32) * step_angle[:, None, None]
    cos_short = jnp.cos(angle_rows).astype(jnp.bfloat16)
    sin_short = jnp.sin(angle_rows).astype(jnp.bfloat16)
    cos_short, sin_short = lax.optimization_barrier((cos_short, sin_short))
    cos_rows = cos_short.astype(jnp.float32)
    sin_rows = sin_short.astype(jnp.float32)
    lane_table = jnp.concatenate([jnp.cos(angle_lanes).astype(jnp.bfloat16), (-jnp.sin(angle_lanes)).astype(jnp.bfloat16)], axis=1)
    limit = jnp.minimum((lengths - 1) // 2, columns - 1)
    keep = wave_numbers[None, :] <= limit[:, None]
    factor = jnp.where(keep, jnp.where(wave_numbers == 0, 1.0, 2.0)[None, :], 0.0).astype(jnp.float32)[None, None, :, None, :]
    real_part = coef[:, 0].astype(jnp.float32)[:, :, :, None, :]
    imag_part = coef[:, 1].astype(jnp.float32)[:, :, :, None, :]
    mixed = jnp.concatenate([factor * (real_part * cos_rows - imag_part * sin_rows), factor * (real_part * sin_rows + imag_part * cos_rows)], axis=-1).astype(jnp.bfloat16)
    grid = jnp.einsum('fhnqc,ncr->fhnqr', mixed.astype(jnp.float32), lane_table.astype(jnp.float32))
    paired = grid.reshape(grid.shape[0] // 2, 2, grid.shape[1], grid.shape[2], row_total, 128)
    inside = (128 * row_index[:, None] + lane_index[None, :])[None] < lengths[:, None, None]
    flux = jnp.where(inside, paired[:, 0] * paired[:, 1], 0.0).astype(jnp.bfloat16)
    back = jnp.einsum('ohnqr,ncr->ohnqc', flux.astype(jnp.float32), lane_table.astype(jnp.float32))
    back_real = back[..., :columns]
    back_imag = back[..., columns:]
    inverse_length = (1.0 / lengths.astype(jnp.float32))[None, None, :, None]
    out_real = lax.optimization_barrier(jnp.sum(cos_rows * back_real + sin_rows * back_imag, axis=3)) * inverse_length
    out_imag = lax.optimization_barrier(jnp.sum(cos_rows * back_imag - sin_rows * back_real, axis=3)) * inverse_length
    result = jnp.stack([out_real, out_imag], axis=1)
    return jnp.where(keep[None, None, None], result, 0.0).astype(jnp.bfloat16)

def reference(spectral_in, legendre, weights, cycle_points, assignment):
    selector = selector_table(assignment, NM)
    masked = selector[:, :, None, :, None, :] * spectral_in[None, None]
    halves = jnp.einsum('pjc,asfpic->afijps', legendre.astype(jnp.float32), masked.astype(jnp.float32))
    north_part = halves[0] + halves[1]
    south_part = halves[0] - halves[1]
    fourier_in = jnp.stack([north_part, south_part], axis=2).reshape(FLD, 2, 2, HALF, NM).astype(jnp.bfloat16)
    wave_numbers = jnp.stack([assignment, NM - 1 - assignment], axis=-1).reshape(NM)
    grid_width = -(-(4 * HALF + 16) // 128) * 128
    cycle_block = 16
    coef_blocks = fourier_in.reshape(FLD, 2, 2, HALF // cycle_block, cycle_block, NM).transpose(3, 0, 1, 2, 4, 5)
    length_blocks = cycle_points.reshape(HALF // cycle_block, cycle_block)

    def one_block(inputs):
        return cycle_transform(inputs[0], inputs[1], wave_numbers, grid_width)
    fourier_out = lax.map(one_block, (coef_blocks, length_blocks))
    fourier_out = fourier_out.transpose(1, 2, 3, 0, 4, 5).reshape(OUT, 2, 2, HALF, NM)
    spread = fourier_out.astype(jnp.float32)
    weight_rows = weights[None, None, :, None]
    even_part = weight_rows * (spread[:, :, 0] + spread[:, :, 1])
    odd_part = weight_rows * (spread[:, :, 0] - spread[:, :, 1])
    mirrored = jnp.stack([even_part, odd_part]).astype(jnp.bfloat16).reshape(2, OUT, 2, HALF, PAIRS, 2)
    partials = jnp.einsum('pjc,aoijps->asopic', legendre.astype(jnp.float32), mirrored.astype(jnp.float32))
    summed = lax.optimization_barrier(jnp.sum(selector.astype(jnp.float32)[:, :, None, :, None, :] * partials, axis=(0, 1)))
    return summed * (math.sqrt(NM) / 2.0)
```

```python
import functools
import math

import jax
import jax.numpy as jnp
from jax import lax
from jax.experimental import pallas as pl
from jax.experimental.pallas import tpu as pltpu
from jax.sharding import PartitionSpec as P

F32 = jnp.float32
BF16 = jnp.bfloat16
VMEM_BYTES = 56 * 1024 * 1024

LANES = 128
ROWS = 11
BAND = 384
COLS = ((0, 128), (128, 384), (384, 512), (512, 768))


def turn(frac):
    x = frac * math.pi
    y = x * x
    s = F32(-1.0 / 39916800.0)
    for c in (1.0 / 362880.0, -1.0 / 5040.0, 1.0 / 120.0, -1.0 / 6.0, 1.0):
        s = s * y + F32(c)
    s = s * x
    c2 = F32(1.0 / 479001600.0)
    for c in (-1.0 / 3628800.0, 1.0 / 40320.0, -1.0 / 720.0, 1.0 / 24.0, -0.5, 1.0):
        c2 = c2 * y + F32(c)
    return 1.0 - 2.0 * s * s, 2.0 * s * c2


def angle(product, length, inverse):
    whole = jnp.floor(product * inverse)
    frac = (product - whole * length) * inverse
    return frac - jnp.where(frac > 0.5, F32(1.0), F32(0.0))


def table_kernel(len_ref, asg_ref, t_ref, a_ref, p_ref, r_scr):
    step = pl.program_id(0)
    length_i = len_ref[step]
    length = length_i.astype(F32)
    inverse = 1.0 / jnp.full((1, 1), length, F32)

    @pl.when(step == 0)
    def _():
        pair = asg_ref[...]
        lane = lax.broadcasted_iota(jnp.int32, (1, 256), 1)
        for t in range(4):
            low = 4 * lane + t
            high = 1279 - 4 * (lane + 128) - t
            p_ref[0, :, 256 * t : 256 * t + 256] = jnp.where(pair == low, F32(1), F32(0)).astype(BF16)
            p_ref[1, :, 256 * t : 256 * t + 256] = jnp.where(pair == high, F32(1), F32(0)).astype(BF16)

    r = lax.broadcasted_iota(jnp.int32, (48, LANES), 1).astype(F32)
    w1 = lax.broadcasted_iota(jnp.int32, (48, LANES), 0).astype(F32)
    rc, rs = turn(angle(32.0 * w1 * r, length, inverse))
    r_scr[0] = rc
    r_scr[1] = rs
    w2 = lax.broadcasted_iota(jnp.int32, (8, LANES), 0).astype(F32)
    r8 = lax.broadcasted_iota(jnp.int32, (8, LANES), 1).astype(F32)
    for t in range(4):
        vc, vs = turn(angle((4.0 * w2 + float(t)) * r8, length, inverse))
        c0 = COLS[t][0]
        for k in range(BAND // 16):
            parts = []
            for e in range(2):
                w = 2 * k + e
                bc = r_scr[0, w : w + 1, :]
                bs = r_scr[1, w : w + 1, :]
                parts.append((bc * vc - bs * vs, bc * vs + bs * vc))
            cc = jnp.concatenate([parts[0][0], parts[1][0]], axis=0).astype(BF16)
            ss = jnp.concatenate([parts[0][1], parts[1][1]], axis=0).astype(BF16)
            t_ref[0, 16 * k : 16 * k + 16, c0 : c0 + LANES] = cc
            t_ref[0, BAND + 16 * k : BAND + 16 * k + 16, c0 : c0 + LANES] = -ss
            if t % 2:
                t_ref[0, 16 * k : 16 * k + 16, c0 + LANES : c0 + 2 * LANES] = ss
                t_ref[0, BAND + 16 * k : BAND + 16 * k + 16, c0 + LANES : c0 + 2 * LANES] = cc

    limit = jnp.minimum((length_i - 1) // 2, 1279)
    for t in range(4):
        w = lax.broadcasted_iota(jnp.int32, (16, BAND), 1)
        m = 4 * w + t
        q = lax.broadcasted_iota(jnp.int32, (16, BAND), 0)
        ac, as_ = turn(angle((m * (LANES * q)).astype(F32), length, inverse))
        keep = m <= limit
        up = jnp.where(keep, jnp.where(m == 0, F32(1), F32(2)), F32(0))
        down = jnp.where(keep, jnp.broadcast_to(inverse, m.shape), F32(0))
        lanes = slice(BAND * t, BAND * t + BAND)
        a_ref[0, 0, :, lanes] = up * ac
        a_ref[0, 1, :, lanes] = up * as_
        a_ref[0, 2, :, lanes] = down * ac
        a_ref[0, 3, :, lanes] = down * as_


def legendre_kernel(pairs, cycles, slots, asg_ref, leg_ref, spec_ref, out_ref, scr):
    p = pl.program_id(0)
    split = 1280 - asg_ref[p]
    column = lax.broadcasted_iota(jnp.int32, (1, 1281), 1)
    second = column >= split
    odd = (jnp.where(second, column - split, column) & 1) == 1
    first_f = jnp.where(second, F32(0), F32(1))
    second_f = jnp.where(second, F32(1), F32(0))
    sign = jnp.where(odd, F32(-1), F32(1))
    spec = spec_ref[0].astype(F32)
    blocks = []
    for seg in (first_f, second_f):
        for i in range(2):
            for e in range(2):
                rows = spec[16 * i + 8 * e : 16 * i + 8 * e + 8]
                blocks.append(rows * seg)
                blocks.append(rows * (seg * sign))
    x = jnp.concatenate(blocks, axis=0).astype(BF16)
    y = lax.dot_general(leg_ref[0], x, (((1,), (1,)), ((), ())), preferred_element_type=F32)

    @pl.when(p == 0)
    def _():
        scr[...] = jnp.zeros_like(scr)

    for jj in range(cycles):
        scr[pl.ds(p * cycles + jj, 64, stride=slots), :] = y[64 * jj : 64 * jj + 64]

    @pl.when(p == pairs - 1)
    def _():
        out_ref[...] = scr[...].reshape(out_ref.shape).astype(BF16)


def grid_kernel(cycles, pairs, slots, back_slots, len_ref, r_ref, p_ref, t_ref, a_ref, out_ref,
                xf, xs, xt, y, m, g, hb, o, pf):
    step = pl.program_id(0)

    @pl.when(step == 0)
    def _():
        xf[...] = r_ref[...].astype(F32).reshape(xf.shape)
        for jj in range(cycles):
            for p in range(pairs):
                xs[64 * p : 64 * p + 64, :] = xf[pl.ds(p * cycles + jj, 64, stride=slots), :]
            turned = xs[...].T.astype(BF16)
            xt[0, 64 * jj : 64 * jj + 64, :] = turned[:64]
            xt[1, 64 * jj : 64 * jj + 64, :] = turned[64:]
        for t in range(4):
            cols = slice(256 * t, 256 * t + 256)
            y0 = jnp.dot(xt[0], p_ref[0, :, cols], preferred_element_type=F32)
            y1 = jnp.dot(xt[1], p_ref[1, :, cols], preferred_element_type=F32)
            y[:, BAND * t : BAND * t + 128] = y0[:, :128]
            y[:, BAND * t + 128 : BAND * t + 256] = y0[:, 128:] + y1[:, :128]
            y[:, BAND * t + 256 : BAND * t + 384] = y1[:, 128:]
        pf[...] = jnp.zeros_like(pf)

    base = pl.multiple_of(step * 64, 64)
    for t in range(4):
        lanes = slice(BAND * t, BAND * t + BAND)
        fr = y[pl.ds(base, 32), lanes]
        fi = y[pl.ds(base + 32, 32), lanes]
        for q in range(ROWS):
            ar = a_ref[0, 0, q : q + 1, lanes]
            ai = a_ref[0, 1, q : q + 1, lanes]
            m[32 * q : 32 * q + 32, :BAND] = (fr * ar - fi * ai).astype(BF16)
            m[32 * q : 32 * q + 32, BAND:] = (fr * ai + fi * ar).astype(BF16)
        lo, hi = COLS[t]
        g[:, lo:hi] = jnp.dot(m[...], t_ref[0, :, lo:hi], preferred_element_type=F32)

    quarter = len_ref[step] // 4
    lane = lax.broadcasted_iota(jnp.int32, (16, LANES), 1)
    for q in range(ROWS):
        rows = slice(32 * q, 32 * q + 32)
        r0, r1, i1 = g[rows, 0:128], g[rows, 128:256], g[rows, 256:384]
        r2, r3, i3 = g[rows, 384:512], g[rows, 512:640], g[rows, 640:768]
        even, turned = r0 + r2, r0 - r2
        odd, skew = r1 + r3, i1 - i3
        inside = lane < quarter - LANES * q
        flux = []
        for value in (even + odd, turned - skew, even - odd, turned + skew):
            flux.append(jnp.where(inside, value[:16] * value[16:], F32(0)))
        f0, f1, f2, f3 = flux
        back_rows = slice(16 * q, 16 * q + 16)
        plus, cross = f0 + f2, f1 + f3
        minus, skew_f = f0 - f2, f1 - f3
        hb[back_rows, 0:128] = (plus + cross).astype(BF16)
        hb[back_rows, 128:256] = minus.astype(BF16)
        hb[back_rows, 256:384] = (-skew_f).astype(BF16)
        hb[back_rows, 384:512] = (plus - cross).astype(BF16)
        hb[back_rows, 512:640] = minus.astype(BF16)
        hb[back_rows, 640:768] = skew_f.astype(BF16)

    out_base = pl.multiple_of(step * 32, 32)
    for t in range(4):
        lanes = slice(BAND * t, BAND * t + BAND)
        lo, hi = COLS[t]
        b = lax.dot_general(hb[:, lo:hi], t_ref[0, :, lo:hi], (((1,), (1,)), ((), ())),
                            preferred_element_type=F32)
        real = jnp.zeros((16, BAND), F32)
        imag = jnp.zeros((16, BAND), F32)
        for q in range(ROWS):
            br = b[16 * q : 16 * q + 16, :BAND]
            bi = b[16 * q : 16 * q + 16, BAND:]
            ar = a_ref[0, 2, q : q + 1, lanes]
            ai = a_ref[0, 3, q : q + 1, lanes]
            real = real + (ar * br + ai * bi)
            imag = imag + (ar * bi - ai * br)
        o[pl.ds(out_base, 16), lanes] = real.astype(BF16)
        o[pl.ds(out_base + 16, 16), lanes] = imag.astype(BF16)

    @pl.when(step == cycles - 1)
    def _():
        tails = []
        for s in range(2):
            total = None
            for t in range(4):
                piece = o[:, BAND * t + 128 * s : BAND * t + 128 * s + 256]
                part = lax.dot_general(p_ref[s, :, 256 * t : 256 * t + 256], piece,
                                       (((1,), (1,)), ((), ())), preferred_element_type=F32)
                total = part if total is None else total + part
            for p in range(pairs):
                pf[pl.ds(3 * p + s, 64, stride=back_slots), :] = total[64 * p : 64 * p + 64, :128]
            tails.append(total[:, 128:])
        last = jnp.concatenate([tails[0], tails[1], jnp.zeros_like(tails[0]), jnp.zeros_like(tails[0])], axis=1)
        for p in range(pairs):
            pf[pl.ds(3 * p + 2, 64, stride=back_slots), :] = last[64 * p : 64 * p + 64]
        out_ref[...] = pf[...].reshape(out_ref.shape).astype(BF16)


def inverse_kernel(back_slots, asg_ref, r_ref, leg_ref, w_ref, out_ref, rf):
    p = pl.program_id(0)

    @pl.when(p == 0)
    def _():
        rf[...] = r_ref[...].astype(F32).reshape(rf.shape)

    weight = w_ref[...]
    blocks = []
    for b in range(3):
        blocks.append(rf[pl.ds(3 * p + b, 64, stride=back_slots), :])
    z = jnp.concatenate(blocks + [jnp.zeros_like(blocks[0])], axis=0).T
    left = []
    for s in range(2):
        cols = [z[32 * jj : 32 * jj + 32, 64 * s : 64 * s + 64] for jj in range(4)]
        cols.append(z[32 * s : 32 * s + 32, 128:192])
        zs = jnp.concatenate(cols, axis=1)
        for par in range(2):
            for i in range(2):
                north = zs[16 * i : 16 * i + 8]
                south = zs[16 * i + 8 : 16 * i + 16]
                left.append(weight * (north + south if par == 0 else north - south))
    lhs = jnp.concatenate(left, axis=0).astype(BF16)
    res = jnp.dot(lhs, leg_ref[0], preferred_element_type=F32)
    split = 1280 - asg_ref[p]
    column = lax.broadcasted_iota(jnp.int32, (1, 1281), 1)
    second = column >= split
    odd = (jnp.where(second, column - split, column) & 1) == 1
    value = jnp.where(
        second,
        jnp.where(odd, res[48:64], res[32:48]),
        jnp.where(odd, res[16:32], res[0:16]),
    )
    out_ref[0] = value.astype(BF16)


def params():
    return pltpu.CompilerParams(vmem_limit_bytes=VMEM_BYTES)


def on_device(spectral_in, legendre, weights, cycle_points, assignment):
    lat = lax.axis_index("lat")
    lev = lax.axis_index("lev")
    pairs, quarter, width = legendre.shape
    cycles = quarter // 64
    slots = 56
    back_slots = 32
    fields = spectral_in.shape[0]

    own = lax.dynamic_slice_in_dim(assignment, lat * pairs, pairs)
    lengths = lax.dynamic_slice_in_dim(cycle_points, lev * quarter, quarter).reshape(cycles, 64)
    lengths = lax.dynamic_index_in_dim(lengths, lat, axis=1, keepdims=False)
    column = assignment.reshape(64, pairs).T.reshape(64 * pairs, 1)

    tables, rows, place = pl.pallas_call(
        table_kernel,
        grid_spec=pltpu.PrefetchScalarGridSpec(
            num_scalar_prefetch=1,
            grid=(cycles,),
            in_specs=[pl.BlockSpec((64 * pairs, 1), lambda i, *_: (0, 0))],
            out_specs=[
                pl.BlockSpec((1, 2 * BAND, 768), lambda i, *_: (i, 0, 0)),
                pl.BlockSpec((1, 4, 16, 4 * BAND), lambda i, *_: (i, 0, 0, 0)),
                pl.BlockSpec((2, 64 * pairs, 1024), lambda i, *_: (0, 0, 0)),
            ],
            scratch_shapes=[pltpu.VMEM((2, 48, LANES), F32)],
        ),
        out_shape=[
            jax.ShapeDtypeStruct((cycles, 2 * BAND, 768), BF16),
            jax.ShapeDtypeStruct((cycles, 4, 16, 4 * BAND), F32),
            jax.ShapeDtypeStruct((2, 64 * pairs, 1024), BF16),
        ],
        compiler_params=params(),
        cost_estimate=pl.CostEstimate(flops=20_000_000, bytes_accessed=16_000_000, transcendentals=0),
    )(lengths, column)

    gathered = lax.all_gather(spectral_in, "lev", axis=0, tiled=False)
    spec = gathered.reshape(4, fields // 2, 2, pairs, 2, width)
    spec = spec.transpose(3, 4, 2, 0, 1, 5).reshape(pairs, 8 * fields, width)

    sent = pl.pallas_call(
        functools.partial(legendre_kernel, pairs, cycles, slots),
        grid_spec=pltpu.PrefetchScalarGridSpec(
            num_scalar_prefetch=1,
            grid=(pairs,),
            in_specs=[
                pl.BlockSpec((1, quarter, width), lambda i, *_: (i, 0, 0)),
                pl.BlockSpec((1, 8 * fields, width), lambda i, *_: (i, 0, 0)),
            ],
            out_specs=pl.BlockSpec((64, slots, 128), lambda i, *_: (0, 0, 0)),
            scratch_shapes=[pltpu.VMEM((64 * slots, 128), F32)],
        ),
        out_shape=jax.ShapeDtypeStruct((64, slots, 128), BF16),
        compiler_params=params(),
        cost_estimate=pl.CostEstimate(flops=1_100_000_000, bytes_accessed=11_000_000, transcendentals=0),
    )(own, legendre, spec)

    received = lax.all_to_all(sent, "lat", split_axis=0, concat_axis=0, tiled=True)

    returned = pl.pallas_call(
        functools.partial(grid_kernel, cycles, pairs, slots, back_slots),
        grid_spec=pltpu.PrefetchScalarGridSpec(
            num_scalar_prefetch=1,
            grid=(cycles,),
            in_specs=[
                pl.BlockSpec((64, slots, 128), lambda i, *_: (0, 0, 0)),
                pl.BlockSpec((2, 64 * pairs, 1024), lambda i, *_: (0, 0, 0)),
                pl.BlockSpec((1, 2 * BAND, 768), lambda i, *_: (i, 0, 0)),
                pl.BlockSpec((1, 4, 16, 4 * BAND), lambda i, *_: (i, 0, 0, 0)),
            ],
            out_specs=pl.BlockSpec((64, back_slots, 128), lambda i, *_: (0, 0, 0)),
            scratch_shapes=[
                pltpu.VMEM((64 * slots, 128), F32),
                pltpu.VMEM((64 * pairs, 128), F32),
                pltpu.VMEM((2, 64 * cycles, 64 * pairs), BF16),
                pltpu.VMEM((64 * cycles, 4 * BAND), F32),
                pltpu.VMEM((32 * ROWS, 2 * BAND), BF16),
                pltpu.VMEM((32 * ROWS, 768), F32),
                pltpu.VMEM((16 * ROWS, 768), BF16),
                pltpu.VMEM((32 * cycles, 4 * BAND), BF16),
                pltpu.VMEM((64 * back_slots, 128), F32),
            ],
        ),
        out_shape=jax.ShapeDtypeStruct((64, back_slots, 128), BF16),
        compiler_params=params(),
        cost_estimate=pl.CostEstimate(flops=5_000_000_000, bytes_accessed=13_000_000, transcendentals=0),
    )(lengths, received, place, tables, rows)

    home = lax.all_to_all(returned, "lat", split_axis=0, concat_axis=0, tiled=True)

    partial = pl.pallas_call(
        functools.partial(inverse_kernel, back_slots),
        grid_spec=pltpu.PrefetchScalarGridSpec(
            num_scalar_prefetch=1,
            grid=(pairs,),
            in_specs=[
                pl.BlockSpec((64, back_slots, 128), lambda i, *_: (0, 0, 0)),
                pl.BlockSpec((1, quarter, width), lambda i, *_: (i, 0, 0)),
                pl.BlockSpec((1, quarter), lambda i, *_: (0, 0)),
            ],
            out_specs=pl.BlockSpec((1, 16, width), lambda i, *_: (i, 0, 0)),
            scratch_shapes=[pltpu.VMEM((64 * back_slots, 128), F32)],
        ),
        out_shape=jax.ShapeDtypeStruct((pairs, 16, width), BF16),
        compiler_params=params(),
        cost_estimate=pl.CostEstimate(flops=600_000_000, bytes_accessed=10_000_000, transcendentals=0),
    )(own, home, legendre, weights.reshape(1, quarter))

    partial = partial.reshape(pairs, 2, 8, width).transpose(2, 0, 1, 3)
    summed = lax.psum_scatter(partial, "lev", scatter_dimension=0, tiled=True).astype(F32)
    return summed * (math.sqrt(width - 1) / 2.0)


def solution(mesh):
    return jax.shard_map(
        on_device,
        mesh=mesh,
        in_specs=(P("lev", "lat", None, None), P("lat", "lev", None), P("lev"), P(), P()),
        out_specs=P("lev", "lat", None, None),
        check_vma=False,
    )
```

```python
import functools
import math

import jax
import jax.numpy as jnp
from jax import lax
from jax.experimental import pallas as pl
from jax.experimental.pallas import tpu as pltpu
from jax.sharding import PartitionSpec as P

F32 = jnp.float32
BF16 = jnp.bfloat16

LANES = 128
ROWS = 11
HALF = 640
AHEAD = 3
SPAN = 384


def turn(frac):
    x = frac * math.pi
    y = x * x
    s = F32(-1.0 / 39916800.0)
    for c in (1.0 / 362880.0, -1.0 / 5040.0, 1.0 / 120.0, -1.0 / 6.0, 1.0):
        s = s * y + F32(c)
    s = s * x
    c2 = F32(1.0 / 479001600.0)
    for c in (-1.0 / 3628800.0, 1.0 / 40320.0, -1.0 / 720.0, 1.0 / 24.0, -0.5, 1.0):
        c2 = c2 * y + F32(c)
    return 1.0 - 2.0 * s * s, 2.0 * s * c2


def angle(product, length, inverse):
    whole = jnp.floor(product * inverse)
    frac = (product - whole * length) * inverse
    return frac - jnp.where(frac > 0.5, F32(1.0), F32(0.0))


def table_kernel(len_ref, asg_ref, t_ref, a_ref, p_ref, r_scr):
    step = pl.program_id(0)
    length_i = len_ref[step]
    length = length_i.astype(F32)
    inverse = 1.0 / jnp.full((1, 1), length, F32)

    @pl.when(step == 0)
    def _():
        pair = asg_ref[...]
        lane = lax.broadcasted_iota(jnp.int32, (1, SPAN), 1)
        for t in range(2):
            low = 2 * lane + t
            high = 1279 - 2 * (lane + HALF - SPAN) - t
            cols = slice(SPAN * t, SPAN * t + SPAN)
            p_ref[0, :, cols] = jnp.where(pair == low, F32(1), F32(0)).astype(BF16)
            p_ref[1, :, cols] = jnp.where(pair == high, F32(1), F32(0)).astype(BF16)

    r = lax.broadcasted_iota(jnp.int32, (HALF // 8, LANES), 1).astype(F32)
    u1 = lax.broadcasted_iota(jnp.int32, (HALF // 8, LANES), 0).astype(F32)
    rc, rs = turn(angle(16.0 * u1 * r, length, inverse))
    r_scr[0] = rc
    r_scr[1] = rs
    u2 = lax.broadcasted_iota(jnp.int32, (8, LANES), 0)
    r8 = lax.broadcasted_iota(jnp.int32, (8, LANES), 1).astype(F32)
    flip8 = jnp.where((u2 & 1) == 1, F32(-1), F32(1))
    flip = jnp.concatenate([flip8, flip8], axis=0)
    for t in range(2):
        vc, vs = turn(angle((2.0 * u2.astype(F32) + float(t)) * r8, length, inverse))
        for k in range(HALF // 16):
            parts = []
            for e in range(2):
                w = 2 * k + e
                bc = r_scr[0, w : w + 1, :]
                bs = r_scr[1, w : w + 1, :]
                parts.append((bc * vc - bs * vs, bc * vs + bs * vc))
            cc = jnp.concatenate([parts[0][0], parts[1][0]], axis=0)
            ss = jnp.concatenate([parts[0][1], parts[1][1]], axis=0)
            top = 2 * HALF * t + 16 * k
            low = top + HALF
            t_ref[0, top : top + 16, :LANES] = cc.astype(BF16)
            t_ref[0, low : low + 16, :LANES] = (-ss).astype(BF16)
            if t == 0:
                t_ref[0, top : top + 16, LANES:] = (flip * cc).astype(BF16)
                t_ref[0, low : low + 16, LANES:] = (-flip * ss).astype(BF16)
            else:
                t_ref[0, top : top + 16, LANES:] = (flip * ss).astype(BF16)
                t_ref[0, low : low + 16, LANES:] = (flip * cc).astype(BF16)

    limit = jnp.minimum((length_i - 1) // 2, 1279)
    for t in range(2):
        m = 2 * lax.broadcasted_iota(jnp.int32, (16, HALF), 1) + t
        q = lax.broadcasted_iota(jnp.int32, (16, HALF), 0)
        ac, as_ = turn(angle((m * (LANES * q)).astype(F32), length, inverse))
        keep = m <= limit
        up = jnp.where(keep, jnp.where(m == 0, F32(1), F32(2)), F32(0))
        down = jnp.where(keep, jnp.broadcast_to(inverse, m.shape), F32(0))
        lanes = slice(HALF * t, HALF * t + HALF)
        a_ref[0, 0, :, lanes] = up * ac
        a_ref[0, 1, :, lanes] = up * as_
        a_ref[0, 2, :, lanes] = down * ac
        a_ref[0, 3, :, lanes] = down * as_


def legendre_kernel(pairs, cycles, slots, asg_ref, leg_hbm, spec_ref, out_ref, scr, xs, leg_all, sems):
    p = pl.program_id(0)

    def fetch(k):
        return pltpu.make_async_copy(leg_hbm.at[k], leg_all.at[k], sems.at[k])

    @pl.when(p == 0)
    def _():
        for k in range(AHEAD):
            fetch(k).start()

    @pl.when(p + AHEAD < pairs)
    def _():
        fetch(p + AHEAD).start()

    split = 1280 - asg_ref[lax.axis_index("lat") * pairs + p]
    column = lax.broadcasted_iota(jnp.int32, (1, 1281), 1)
    second = column >= split
    odd = (jnp.where(second, column - split, column) & 1) == 1
    first_f = jnp.where(second, F32(0), F32(1))
    second_f = jnp.where(second, F32(1), F32(0))
    sign = jnp.where(odd, F32(-1), F32(1))
    for f in range(16):
        o, e = f // 2, f % 2
        pair = spec_ref[f, p].astype(F32)
        xs[8 * e + o : 8 * e + o + 1, :] = pair[:1]
        xs[16 + 8 * e + o : 17 + 8 * e + o, :] = pair[1:]
    spec = xs[...]
    blocks = []
    for seg in (first_f, second_f):
        for i in range(2):
            for e in range(2):
                rows = spec[16 * i + 8 * e : 16 * i + 8 * e + 8]
                blocks.append(rows * seg)
                blocks.append(rows * (seg * sign))
    x = jnp.concatenate(blocks, axis=0)
    last = jnp.broadcast_to(x[:, 1280:], (128, 128)).T[:1]
    x = x[:, :1280].astype(BF16)
    fetch(p).wait()
    y = lax.dot_general(leg_all[p, :, :1280], x, (((1,), (1,)), ((), ())), preferred_element_type=F32)
    y = y + leg_all[p, :, 1280:].astype(F32) * last

    for jj in range(cycles):
        scr[pl.ds(p * cycles + jj, 64, stride=slots), :] = y[64 * jj : 64 * jj + 64]

    @pl.when(p == pairs - 1)
    def _():
        out_ref[...] = scr[: 64 * slots].reshape(out_ref.shape).astype(BF16)


def grid_kernel(cycles, pairs, slots, back_slots, len_ref, r_ref, p_hbm, t_hbm, a_hbm, out_ref,
                xf, xs, xt, y, m, g, hb, o, pf, p_ref, t_all, a_all, sems):
    step = pl.program_id(0)

    def table_copies(k):
        return (
            pltpu.make_async_copy(t_hbm.at[k], t_all.at[k], sems.at[k]),
            pltpu.make_async_copy(a_hbm.at[k], a_all.at[k], sems.at[cycles + k]),
        )

    place_copy = pltpu.make_async_copy(p_hbm, p_ref, sems.at[2 * cycles])

    @pl.when(step == 0)
    def _():
        place_copy.start()
        for copy in table_copies(0):
            copy.start()
        xf[: 64 * slots] = r_ref[...].astype(F32).reshape(64 * slots, 128)
        for jj in range(cycles):
            for p in range(pairs):
                xs[64 * p : 64 * p + 64, :] = xf[pl.ds(p * cycles + jj, 64, stride=slots), :]
            turned = xs[...].T.astype(BF16)
            xt[0, 64 * jj : 64 * jj + 64, :] = turned[:64]
            xt[1, 64 * jj : 64 * jj + 64, :] = turned[64:]
        place_copy.wait()
        for t in range(2):
            cols = slice(SPAN * t, SPAN * t + SPAN)
            y0 = jnp.dot(xt[0], p_ref[0, :, cols], preferred_element_type=F32)
            y1 = jnp.dot(xt[1], p_ref[1, :, cols], preferred_element_type=F32)
            y[:, HALF * t : HALF * t + 256] = y0[:, :256]
            y[:, HALF * t + 256 : HALF * t + 384] = y0[:, 256:] + y1[:, :128]
            y[:, HALF * t + 384 : HALF * t + 640] = y1[:, 128:]

    @pl.when(step + 1 < cycles)
    def _():
        for copy in table_copies(step + 1):
            copy.start()

    for copy in table_copies(step):
        copy.wait()
    t_ref, a_ref = t_all.at[step], a_all.at[step]
    base = pl.multiple_of(step * 64, 64)
    for t in range(2):
        lanes = slice(HALF * t, HALF * t + HALF)
        fr = y[pl.ds(base, 32), lanes]
        fi = y[pl.ds(base + 32, 32), lanes]
        for q in range(ROWS):
            ar = a_ref[0, q : q + 1, lanes]
            ai = a_ref[1, q : q + 1, lanes]
            m[t, 32 * q : 32 * q + 32, :HALF] = (fr * ar - fi * ai).astype(BF16)
            m[t, 32 * q : 32 * q + 32, HALF:] = (fr * ai + fi * ar).astype(BF16)
        g[:, 256 * t : 256 * t + 256] = jnp.dot(
            m[t], t_ref[2 * HALF * t : 2 * HALF * t + 2 * HALF, :], preferred_element_type=F32
        )

    quarter = len_ref[step] // 4
    lane = lax.broadcasted_iota(jnp.int32, (16, LANES), 1)
    for q in range(ROWS):
        rows = slice(32 * q, 32 * q + 32)
        even, turned = g[rows, 0:128], g[rows, 128:256]
        odd, skew = g[rows, 256:384], g[rows, 384:512]
        inside = lane < quarter - LANES * q
        flux = []
        for value in (even + odd, turned - skew, even - odd, turned + skew):
            flux.append(jnp.where(inside, value[:16] * value[16:], F32(0)))
        f0, f1, f2, f3 = flux
        back_rows = slice(16 * q, 16 * q + 16)
        hb[back_rows, 0:128] = (f0 + f2).astype(BF16)
        hb[back_rows, 128:256] = (f1 + f3).astype(BF16)
        hb[back_rows, 256:384] = (f0 - f2).astype(BF16)
        hb[back_rows, 384:512] = (f3 - f1).astype(BF16)

    out_base = pl.multiple_of(step * 32, 32)
    for t in range(2):
        lanes = slice(HALF * t, HALF * t + HALF)
        b = lax.dot_general(hb[:, 256 * t : 256 * t + 256], t_ref[2 * HALF * t : 2 * HALF * t + 2 * HALF, :],
                            (((1,), (1,)), ((), ())), preferred_element_type=F32)
        real = jnp.zeros((16, HALF), F32)
        imag = jnp.zeros((16, HALF), F32)
        for q in range(ROWS):
            br = b[16 * q : 16 * q + 16, :HALF]
            bi = b[16 * q : 16 * q + 16, HALF:]
            ar = a_ref[2, q : q + 1, lanes]
            ai = a_ref[3, q : q + 1, lanes]
            real = real + (ar * br + ai * bi)
            imag = imag + (ar * bi - ai * br)
        for k in range(HALF // 128):
            sub = slice(128 * k, 128 * k + 128)
            tile = (5 * t + k) * 32 * cycles
            o[pl.ds(tile + out_base, 16, stride=2), :] = real[:, sub]
            o[pl.ds(tile + out_base + 1, 16, stride=2), :] = imag[:, sub]

    @pl.when(step == cycles - 1)
    def _():
        tails = []
        size = 32 * cycles
        for s in range(2):
            total = None
            for t in range(2):
                tile = (5 * t + 2 * s) * size
                piece = jnp.concatenate(
                    [o[tile + size * k : tile + size * k + size, :] for k in range(3)], axis=1
                ).astype(BF16)
                part = lax.dot_general(p_ref[s, :, SPAN * t : SPAN * t + SPAN], piece,
                                       (((1,), (1,)), ((), ())), preferred_element_type=F32)
                total = part if total is None else total + part
            for p in range(pairs):
                pf[pl.ds(2 * p + s, 64, stride=back_slots), :] = total[64 * p : 64 * p + 64, :128]
            tails.append(total[:, 128:])
        both = jnp.concatenate(tails, axis=1)
        for k in range(pairs // 2):
            pf[pl.ds(2 * pairs + k, 64, stride=back_slots), :] = jnp.concatenate(
                [both[128 * k : 128 * k + 64], both[128 * k + 64 : 128 * k + 128]], axis=1
            )
        if back_slots > 5 * pairs // 2:
            pf[pl.ds(back_slots - 1, 64, stride=back_slots), :] = jnp.zeros((64, 128), F32)
        out_ref[...] = pf[: 64 * back_slots].reshape(out_ref.shape).astype(BF16)


def inverse_kernel(pairs, first, back_slots, asg_ref, r_ref, leg_hbm, w_ref, *rest):
    outs, (rf, vals, leg_all, sems) = rest[:4], rest[4:]
    step = pl.program_id(0)
    p = step + first

    def fetch(k):
        return pltpu.make_async_copy(leg_hbm.at[first + k], leg_all.at[k], sems.at[k])

    @pl.when(step == 0)
    def _():
        for k in range(AHEAD):
            fetch(k).start()
        rf[: 64 * back_slots] = r_ref[...].astype(F32).reshape(64 * back_slots, 128)

    @pl.when(step + AHEAD < pairs // 2)
    def _():
        fetch(step + AHEAD).start()

    weight = w_ref[...]
    blocks = []
    for b in (2 * p, 2 * p + 1, 2 * pairs + p // 2):
        blocks.append(rf[pl.ds(b, 64, stride=back_slots), :])
    z = jnp.concatenate(blocks + [jnp.zeros_like(blocks[0])], axis=0).T
    late = jnp.where(p % 2 == 0, z[:64, 128:192], z[64:, 128:192])
    left = []
    for s in range(2):
        cols = [z[32 * jj : 32 * jj + 32, 64 * s : 64 * s + 64] for jj in range(4)]
        cols.append(late[32 * s : 32 * s + 32])
        zs = jnp.concatenate(cols, axis=1)
        north, south = zs[:16], zs[16:]
        left.append(weight * (north + south))
        left.append(weight * (north - south))
    lhs = jnp.concatenate(left, axis=0).astype(BF16)
    fetch(step).wait()
    res = jnp.dot(lhs, leg_all[step], preferred_element_type=F32)
    split = 1280 - asg_ref[lax.axis_index("lat") * pairs + p]
    column = lax.broadcasted_iota(jnp.int32, (1, 1281), 1)
    second = column >= split
    odd = (jnp.where(second, column - split, column) & 1) == 1
    value = jnp.where(
        second,
        jnp.where(odd, res[48:64], res[32:48]),
        jnp.where(odd, res[16:32], res[0:16]),
    )
    for v in range(4):
        vals[v] = value[4 * v : 4 * v + 4]
    lev = lax.axis_index("lev")
    for k in range(4):
        rows = vals[lax.rem(lev + k, 4)].astype(BF16)
        outs[k][0, step] = rows[:2]
        outs[k][1, step] = rows[2:]


def params(mib):
    return pltpu.CompilerParams(vmem_limit_bytes=int(mib * 1024 * 1024))


def on_device(spectral_in, legendre, weights, cycle_points, assignment):
    lat = lax.axis_index("lat")
    lev = lax.axis_index("lev")
    pairs, quarter, width = legendre.shape
    cycles = quarter // 64
    slots = 50
    back_slots = 26
    fields = spectral_in.shape[0]

    lengths = lax.dynamic_slice_in_dim(cycle_points, lev * quarter, quarter).reshape(cycles, 64)
    lengths = lax.dynamic_index_in_dim(lengths, lat, axis=1, keepdims=False)
    column = assignment.reshape(64, pairs).T.reshape(64 * pairs, 1)

    tables, rows, place = pl.pallas_call(
        table_kernel,
        grid_spec=pltpu.PrefetchScalarGridSpec(
            num_scalar_prefetch=1,
            grid=(cycles,),
            in_specs=[pl.BlockSpec((64 * pairs, 1), lambda i, *_: (0, 0))],
            out_specs=[
                pl.BlockSpec((1, 4 * HALF, 256), lambda i, *_: (i, 0, 0)),
                pl.BlockSpec((1, 4, 16, 2 * HALF), lambda i, *_: (i, 0, 0, 0)),
                pl.BlockSpec((2, 64 * pairs, 2 * SPAN), lambda i, *_: (0, 0, 0)),
            ],
            scratch_shapes=[pltpu.VMEM((2, HALF // 8, LANES), F32)],
        ),
        out_shape=[
            jax.ShapeDtypeStruct((cycles, 4 * HALF, 256), BF16),
            jax.ShapeDtypeStruct((cycles, 4, 16, 2 * HALF), F32),
            jax.ShapeDtypeStruct((2, 64 * pairs, 2 * SPAN), BF16),
        ],
        compiler_params=params(61),
        cost_estimate=pl.CostEstimate(flops=20_000_000, bytes_accessed=16_000_000, transcendentals=0),
    )(lengths, column)

    gathered = lax.all_gather(spectral_in, "lev", axis=0, tiled=True)

    sent = pl.pallas_call(
        functools.partial(legendre_kernel, pairs, cycles, slots),
        grid_spec=pltpu.PrefetchScalarGridSpec(
            num_scalar_prefetch=1,
            grid=(pairs,),
            in_specs=[
                pl.BlockSpec(memory_space=pltpu.HBM),
                pl.BlockSpec((4 * fields, pairs, 2, width), lambda i, *_: (0, 0, 0, 0)),
            ],
            out_specs=pl.BlockSpec((64, slots // 2, 2, 128), lambda i, *_: (0, 0, 0, 0)),
            scratch_shapes=[
                pltpu.VMEM((64 * slots + 56, 128), F32),
                pltpu.VMEM((32, width), F32),
                pltpu.VMEM((pairs, quarter, width), BF16),
                pltpu.SemaphoreType.DMA((pairs,)),
            ],
        ),
        out_shape=jax.ShapeDtypeStruct((64, slots // 2, 2, 128), BF16),
        compiler_params=params(52),
        cost_estimate=pl.CostEstimate(flops=1_100_000_000, bytes_accessed=11_000_000, transcendentals=0),
    )(assignment, legendre, gathered)

    received = lax.all_to_all(sent, "lat", split_axis=0, concat_axis=0, tiled=True)

    returned = pl.pallas_call(
        functools.partial(grid_kernel, cycles, pairs, slots, back_slots),
        grid_spec=pltpu.PrefetchScalarGridSpec(
            num_scalar_prefetch=1,
            grid=(cycles,),
            in_specs=[
                pl.BlockSpec((64, slots // 2, 2, 128), lambda i, *_: (0, 0, 0, 0)),
                pl.BlockSpec(memory_space=pltpu.HBM),
                pl.BlockSpec(memory_space=pltpu.HBM),
                pl.BlockSpec(memory_space=pltpu.HBM),
            ],
            out_specs=pl.BlockSpec((64, back_slots // 2, 2, 128), lambda i, *_: (0, 0, 0, 0)),
            scratch_shapes=[
                pltpu.VMEM((64 * slots + 56, 128), F32),
                pltpu.VMEM((64 * pairs, 128), F32),
                pltpu.VMEM((2, 64 * cycles, 64 * pairs), BF16),
                pltpu.VMEM((64 * cycles, 2 * HALF), F32),
                pltpu.VMEM((2, 32 * ROWS, 2 * HALF), BF16),
                pltpu.VMEM((32 * ROWS, 512), F32),
                pltpu.VMEM((16 * ROWS, 512), BF16),
                pltpu.VMEM((10 * 32 * cycles + 8, 128), F32),
                pltpu.VMEM((64 * back_slots + 32, 128), F32),
                pltpu.VMEM((2, 64 * pairs, 2 * SPAN), BF16),
                pltpu.VMEM((cycles, 4 * HALF, 256), BF16),
                pltpu.VMEM((cycles, 4, 16, 2 * HALF), F32),
                pltpu.SemaphoreType.DMA((2 * cycles + 1,)),
            ],
        ),
        out_shape=jax.ShapeDtypeStruct((64, back_slots // 2, 2, 128), BF16),
        compiler_params=params(59.4),
        cost_estimate=pl.CostEstimate(flops=5_000_000_000, bytes_accessed=13_000_000, transcendentals=0),
    )(lengths, received, place, tables, rows)

    home = lax.all_to_all(returned, "lat", split_axis=0, concat_axis=0, tiled=True)

    parts = []
    for first in range(0, pairs, pairs // 2):
        half = pairs // 2
        blocks = pl.pallas_call(
            functools.partial(inverse_kernel, pairs, first, back_slots),
            grid_spec=pltpu.PrefetchScalarGridSpec(
                num_scalar_prefetch=1,
                grid=(half,),
                in_specs=[
                    pl.BlockSpec((64, back_slots // 2, 2, 128), lambda i, *_: (0, 0, 0, 0)),
                    pl.BlockSpec(memory_space=pltpu.HBM),
                    pl.BlockSpec((1, quarter), lambda i, *_: (0, 0)),
                ],
                out_specs=[pl.BlockSpec((2, half, 2, width), lambda i, *_: (0, 0, 0, 0))] * 4,
                scratch_shapes=[
                    pltpu.VMEM((64 * back_slots + 32, 128), F32),
                    pltpu.VMEM((4, 4, width), F32),
                    pltpu.VMEM((half, quarter, width), BF16),
                    pltpu.SemaphoreType.DMA((half,)),
                ],
            ),
            out_shape=[jax.ShapeDtypeStruct((2, half, 2, width), BF16)] * 4,
            compiler_params=params(52),
            cost_estimate=pl.CostEstimate(flops=300_000_000, bytes_accessed=5_000_000, transcendentals=0),
        )(assignment, home, legendre, weights.reshape(1, quarter))
        total = blocks[0].astype(F32)
        for k in range(1, 4):
            came = lax.ppermute(blocks[k], "lev", [(i, (i + k) % 4) for i in range(4)])
            total = total + came.astype(F32)
        parts.append(total)
    return jnp.concatenate(parts, axis=1) * (math.sqrt(width - 1) / 2.0)


def solution(mesh):
    return jax.shard_map(
        on_device,
        mesh=mesh,
        in_specs=(P("lev", "lat", None, None), P("lat", "lev", None), P("lev"), P(), P()),
        out_specs=P("lev", "lat", None, None),
        check_vma=False,
    )
```

```python
import functools
import math

import jax
import jax.numpy as jnp
from jax import lax
from jax.experimental import pallas as pl
from jax.experimental.pallas import tpu as pltpu
from jax.sharding import PartitionSpec as P

F32 = jnp.float32
BF16 = jnp.bfloat16

LANES = 128
ROWS = 11
HALF = 640
AHEAD = 3
SPAN = 384


def turn(frac):
    x = frac * math.pi
    y = x * x
    s = F32(-1.0 / 39916800.0)
    for c in (1.0 / 362880.0, -1.0 / 5040.0, 1.0 / 120.0, -1.0 / 6.0, 1.0):
        s = s * y + F32(c)
    s = s * x
    c2 = F32(1.0 / 479001600.0)
    for c in (-1.0 / 3628800.0, 1.0 / 40320.0, -1.0 / 720.0, 1.0 / 24.0, -0.5, 1.0):
        c2 = c2 * y + F32(c)
    return 1.0 - 2.0 * s * s, 2.0 * s * c2


def angle(product, length, inverse):
    whole = jnp.floor(product * inverse)
    frac = (product - whole * length) * inverse
    return frac - jnp.where(frac > 0.5, F32(1.0), F32(0.0))


def cycle_length(points_ref, cycles, step):
    return points_ref[lax.axis_index("lev") * (64 * cycles) + 64 * step + lax.axis_index("lat")]


def table_kernel(cycles, pairs, points_ref, asg_ref, spec_ref, t_ref, a_ref, p_ref, own_ref, asg_out, r_scr, col_scr):
    step = pl.program_id(0)
    length_i = cycle_length(points_ref, cycles, step)
    length = length_i.astype(F32)
    inverse = 1.0 / jnp.full((1, 1), length, F32)

    @pl.when(step == 0)
    def _():
        own_ref[...] = spec_ref[...]
        asg_out[...] = asg_ref[...]
        for k in range(pairs // 2):
            row = asg_ref[k : k + 1, :].astype(F32)
            col_scr[128 * k : 128 * k + 128, :] = jnp.broadcast_to(row, (128, 128)).T
        lane = lax.broadcasted_iota(jnp.int32, (1, 128), 1).astype(F32)
        for p in range(pairs):
            pair = col_scr[pl.ds(p, 64, stride=pairs), :]
            for t in range(2):
                for k in range(SPAN // 128):
                    low = 2.0 * (lane + 128.0 * k) + float(t)
                    high = 1279.0 - 2.0 * (lane + float(HALF - SPAN + 128 * k)) - float(t)
                    rows = slice(64 * p, 64 * p + 64)
                    cols = slice(SPAN * t + 128 * k, SPAN * t + 128 * k + 128)
                    p_ref[0, rows, cols] = jnp.where(pair == low, F32(1), F32(0)).astype(BF16)
                    p_ref[1, rows, cols] = jnp.where(pair == high, F32(1), F32(0)).astype(BF16)

    r = lax.broadcasted_iota(jnp.int32, (HALF // 8, LANES), 1).astype(F32)
    u1 = lax.broadcasted_iota(jnp.int32, (HALF // 8, LANES), 0).astype(F32)
    rc, rs = turn(angle(16.0 * u1 * r, length, inverse))
    r_scr[0] = rc
    r_scr[1] = rs
    u2 = lax.broadcasted_iota(jnp.int32, (8, LANES), 0)
    r8 = lax.broadcasted_iota(jnp.int32, (8, LANES), 1).astype(F32)
    flip8 = jnp.where((u2 & 1) == 1, F32(-1), F32(1))
    flip = jnp.concatenate([flip8, flip8], axis=0)
    for t in range(2):
        vc, vs = turn(angle((2.0 * u2.astype(F32) + float(t)) * r8, length, inverse))
        for k in range(HALF // 16):
            parts = []
            for e in range(2):
                w = 2 * k + e
                bc = r_scr[0, w : w + 1, :]
                bs = r_scr[1, w : w + 1, :]
                parts.append((bc * vc - bs * vs, bc * vs + bs * vc))
            cc = jnp.concatenate([parts[0][0], parts[1][0]], axis=0)
            ss = jnp.concatenate([parts[0][1], parts[1][1]], axis=0)
            top = 2 * HALF * t + 16 * k
            low = top + HALF
            t_ref[0, top : top + 16, :LANES] = cc.astype(BF16)
            t_ref[0, low : low + 16, :LANES] = (-ss).astype(BF16)
            if t == 0:
                t_ref[0, top : top + 16, LANES:] = (flip * cc).astype(BF16)
                t_ref[0, low : low + 16, LANES:] = (-flip * ss).astype(BF16)
            else:
                t_ref[0, top : top + 16, LANES:] = (flip * ss).astype(BF16)
                t_ref[0, low : low + 16, LANES:] = (flip * cc).astype(BF16)

    limit = jnp.minimum((length_i - 1) // 2, 1279)
    for t in range(2):
        m = 2 * lax.broadcasted_iota(jnp.int32, (16, HALF), 1) + t
        q = lax.broadcasted_iota(jnp.int32, (16, HALF), 0)
        ac, as_ = turn(angle((m * (LANES * q)).astype(F32), length, inverse))
        keep = m <= limit
        up = jnp.where(keep, jnp.where(m == 0, F32(1), F32(2)), F32(0))
        down = jnp.where(keep, jnp.broadcast_to(inverse, m.shape), F32(0))
        lanes = slice(HALF * t, HALF * t + HALF)
        a_ref[0, 0, :, lanes] = up * ac
        a_ref[0, 1, :, lanes] = up * as_
        a_ref[0, 2, :, lanes] = down * ac
        a_ref[0, 3, :, lanes] = down * as_


def legendre_kernel(pairs, cycles, slots, asg_ref, leg_hbm, *rest):
    specs, (out_ref, scr, xs, leg_all, sems) = rest[:4], rest[4:]
    p = pl.program_id(0)

    def fetch(k):
        return pltpu.make_async_copy(leg_hbm.at[k], leg_all.at[k], sems.at[k])

    @pl.when(p == 0)
    def _():
        for k in range(AHEAD):
            fetch(k).start()

    @pl.when(p + AHEAD < pairs)
    def _():
        fetch(p + AHEAD).start()

    place = lax.axis_index("lat") * pairs + p
    split = 1280 - asg_ref[place // 128, place % 128]
    column = lax.broadcasted_iota(jnp.int32, (1, 1281), 1)
    second = column >= split
    odd = (jnp.where(second, column - split, column) & 1) == 1
    first_f = jnp.where(second, F32(0), F32(1))
    second_f = jnp.where(second, F32(1), F32(0))
    sign = jnp.where(odd, F32(-1), F32(1))
    for f in range(16):
        o, e = f // 2, f % 2
        pair = specs[f // 4][f % 4, p].astype(F32)
        xs[8 * e + o : 8 * e + o + 1, :] = pair[:1]
        xs[16 + 8 * e + o : 17 + 8 * e + o, :] = pair[1:]
    spec = xs[...]
    blocks = []
    for seg in (first_f, second_f):
        for i in range(2):
            for e in range(2):
                rows = spec[16 * i + 8 * e : 16 * i + 8 * e + 8]
                blocks.append(rows * seg)
                blocks.append(rows * (seg * sign))
    x = jnp.concatenate(blocks, axis=0)
    last = jnp.broadcast_to(x[:, 1280:], (128, 128)).T[:1]
    x = x[:, :1280].astype(BF16)
    fetch(p).wait()
    y = lax.dot_general(leg_all[p, :, :1280], x, (((1,), (1,)), ((), ())), preferred_element_type=F32)
    y = y + leg_all[p, :, 1280:].astype(F32) * last

    for jj in range(cycles):
        scr[pl.ds(p * cycles + jj, 64, stride=slots), :] = y[64 * jj : 64 * jj + 64]

    @pl.when(p == pairs - 1)
    def _():
        out_ref[...] = scr[: 64 * slots].reshape(out_ref.shape).astype(BF16)


def grid_kernel(cycles, pairs, slots, back_slots, points_ref, r_ref, p_hbm, t_hbm, a_hbm, out_ref,
                xf, xs, xt, y, m, g, hb, o, pf, p_ref, t_all, a_all, sems):
    step = pl.program_id(0)

    def table_copies(k):
        return (
            pltpu.make_async_copy(t_hbm.at[k], t_all.at[k], sems.at[k]),
            pltpu.make_async_copy(a_hbm.at[k], a_all.at[k], sems.at[cycles + k]),
        )

    place_copy = pltpu.make_async_copy(p_hbm, p_ref, sems.at[2 * cycles])

    @pl.when(step == 0)
    def _():
        place_copy.start()
        for copy in table_copies(0):
            copy.start()
        xf[: 64 * slots] = r_ref[...].astype(F32).reshape(64 * slots, 128)
        for jj in range(cycles):
            for p in range(pairs):
                xs[64 * p : 64 * p + 64, :] = xf[pl.ds(p * cycles + jj, 64, stride=slots), :]
            turned = xs[...].T.astype(BF16)
            xt[0, 64 * jj : 64 * jj + 64, :] = turned[:64]
            xt[1, 64 * jj : 64 * jj + 64, :] = turned[64:]
        place_copy.wait()
        for t in range(2):
            cols = slice(SPAN * t, SPAN * t + SPAN)
            y0 = jnp.dot(xt[0], p_ref[0, :, cols], preferred_element_type=F32)
            y1 = jnp.dot(xt[1], p_ref[1, :, cols], preferred_element_type=F32)
            y[:, HALF * t : HALF * t + 256] = y0[:, :256]
            y[:, HALF * t + 256 : HALF * t + 384] = y0[:, 256:] + y1[:, :128]
            y[:, HALF * t + 384 : HALF * t + 640] = y1[:, 128:]

    @pl.when(step + 1 < cycles)
    def _():
        for copy in table_copies(step + 1):
            copy.start()

    for copy in table_copies(step):
        copy.wait()
    t_ref, a_ref = t_all.at[step], a_all.at[step]
    base = pl.multiple_of(step * 64, 64)
    for t in range(2):
        lanes = slice(HALF * t, HALF * t + HALF)
        fr = y[pl.ds(base, 32), lanes]
        fi = y[pl.ds(base + 32, 32), lanes]
        for q in range(ROWS):
            ar = a_ref[0, q : q + 1, lanes]
            ai = a_ref[1, q : q + 1, lanes]
            m[t, 32 * q : 32 * q + 32, :HALF] = (fr * ar - fi * ai).astype(BF16)
            m[t, 32 * q : 32 * q + 32, HALF:] = (fr * ai + fi * ar).astype(BF16)
        g[:, 256 * t : 256 * t + 256] = jnp.dot(
            m[t], t_ref[2 * HALF * t : 2 * HALF * t + 2 * HALF, :], preferred_element_type=F32
        )

    quarter = cycle_length(points_ref, cycles, step) // 4
    lane = lax.broadcasted_iota(jnp.int32, (16, LANES), 1)
    for q in range(ROWS):
        rows = slice(32 * q, 32 * q + 32)
        even, turned = g[rows, 0:128], g[rows, 128:256]
        odd, skew = g[rows, 256:384], g[rows, 384:512]
        inside = lane < quarter - LANES * q
        flux = []
        for value in (even + odd, turned - skew, even - odd, turned + skew):
            flux.append(jnp.where(inside, value[:16] * value[16:], F32(0)))
        f0, f1, f2, f3 = flux
        back_rows = slice(16 * q, 16 * q + 16)
        hb[back_rows, 0:128] = (f0 + f2).astype(BF16)
        hb[back_rows, 128:256] = (f1 + f3).astype(BF16)
        hb[back_rows, 256:384] = (f0 - f2).astype(BF16)
        hb[back_rows, 384:512] = (f3 - f1).astype(BF16)

    out_base = pl.multiple_of(step * 32, 32)
    for t in range(2):
        lanes = slice(HALF * t, HALF * t + HALF)
        b = lax.dot_general(hb[:, 256 * t : 256 * t + 256], t_ref[2 * HALF * t : 2 * HALF * t + 2 * HALF, :],
                            (((1,), (1,)), ((), ())), preferred_element_type=F32)
        real = jnp.zeros((16, HALF), F32)
        imag = jnp.zeros((16, HALF), F32)
        for q in range(ROWS):
            br = b[16 * q : 16 * q + 16, :HALF]
            bi = b[16 * q : 16 * q + 16, HALF:]
            ar = a_ref[2, q : q + 1, lanes]
            ai = a_ref[3, q : q + 1, lanes]
            real = real + (ar * br + ai * bi)
            imag = imag + (ar * bi - ai * br)
        for k in range(HALF // 128):
            sub = slice(128 * k, 128 * k + 128)
            tile = (5 * t + k) * 32 * cycles
            o[pl.ds(tile + out_base, 16, stride=2), :] = real[:, sub]
            o[pl.ds(tile + out_base + 1, 16, stride=2), :] = imag[:, sub]

    @pl.when(step == cycles - 1)
    def _():
        tails = []
        size = 32 * cycles
        for s in range(2):
            total = None
            for t in range(2):
                tile = (5 * t + 2 * s) * size
                piece = jnp.concatenate(
                    [o[tile + size * k : tile + size * k + size, :] for k in range(3)], axis=1
                ).astype(BF16)
                part = lax.dot_general(p_ref[s, :, SPAN * t : SPAN * t + SPAN], piece,
                                       (((1,), (1,)), ((), ())), preferred_element_type=F32)
                total = part if total is None else total + part
            for p in range(pairs):
                pf[pl.ds(2 * p + s, 64, stride=back_slots), :] = total[64 * p : 64 * p + 64, :128]
            tails.append(total[:, 128:])
        both = jnp.concatenate(tails, axis=1)
        for k in range(pairs // 2):
            pf[pl.ds(2 * pairs + k, 64, stride=back_slots), :] = jnp.concatenate(
                [both[128 * k : 128 * k + 64], both[128 * k + 64 : 128 * k + 128]], axis=1
            )
        if back_slots > 5 * pairs // 2:
            pf[pl.ds(back_slots - 1, 64, stride=back_slots), :] = jnp.zeros((64, 128), F32)
        out_ref[...] = pf[: 64 * back_slots].reshape(out_ref.shape).astype(BF16)


def inverse_kernel(pairs, first, back_slots, asg_ref, r_ref, leg_hbm, w_ref, *rest):
    outs, (rf, leg_all, sems) = rest[:4], rest[4:]
    step = pl.program_id(0)
    p = step + first

    def fetch(k):
        return pltpu.make_async_copy(leg_hbm.at[first + k], leg_all.at[k], sems.at[k])

    @pl.when(step == 0)
    def _():
        for k in range(AHEAD):
            fetch(k).start()
        rf[: 64 * back_slots] = r_ref[...].astype(F32).reshape(64 * back_slots, 128)

    @pl.when(step + AHEAD < pairs // 2)
    def _():
        fetch(step + AHEAD).start()

    weight = w_ref[...]
    blocks = []
    for b in (2 * p, 2 * p + 1, 2 * pairs + p // 2):
        blocks.append(rf[pl.ds(b, 64, stride=back_slots), :])
    z = jnp.concatenate(blocks + [jnp.zeros_like(blocks[0])], axis=0).T
    late = jnp.where(p % 2 == 0, z[:64, 128:192], z[64:, 128:192])
    left = []
    for s in range(2):
        cols = [z[32 * jj : 32 * jj + 32, 64 * s : 64 * s + 64] for jj in range(4)]
        cols.append(late[32 * s : 32 * s + 32])
        zs = jnp.concatenate(cols, axis=1)
        north, south = zs[:16], zs[16:]
        left.append(weight * (north + south))
        left.append(weight * (north - south))
    lhs = jnp.concatenate(left, axis=0).astype(BF16)
    fetch(step).wait()
    res = jnp.dot(lhs, leg_all[step], preferred_element_type=F32)
    split = 1280 - asg_ref[lax.axis_index("lat") * pairs + p]
    column = lax.broadcasted_iota(jnp.int32, (1, 1281), 1)
    second = column >= split
    odd = (jnp.where(second, column - split, column) & 1) == 1
    value = jnp.where(
        second,
        jnp.where(odd, res[48:64], res[32:48]),
        jnp.where(odd, res[16:32], res[0:16]),
    )
    for k in range(4):
        rows = value[4 * k : 4 * k + 4].astype(BF16)
        outs[k][0, step] = rows[:2]
        outs[k][1, step] = rows[2:]


def params(mib):
    return pltpu.CompilerParams(vmem_limit_bytes=int(mib * 1024 * 1024))


def on_device(spectral_in, legendre, weights, cycle_points, assignment):
    pairs, quarter, width = legendre.shape
    cycles = quarter // 64
    slots = 50
    back_slots = 26
    fields = spectral_in.shape[0]

    tables, rows, place, own, held = pl.pallas_call(
        functools.partial(table_kernel, cycles, pairs),
        grid_spec=pltpu.PrefetchScalarGridSpec(
            num_scalar_prefetch=1,
            grid=(cycles,),
            in_specs=[
                pl.BlockSpec((pairs // 2, 128), lambda i, *_: (0, 0)),
                pl.BlockSpec((fields, pairs, 2, width), lambda i, *_: (0, 0, 0, 0)),
            ],
            out_specs=[
                pl.BlockSpec((1, 4 * HALF, 256), lambda i, *_: (i, 0, 0)),
                pl.BlockSpec((1, 4, 16, 2 * HALF), lambda i, *_: (i, 0, 0, 0)),
                pl.BlockSpec((2, 64 * pairs, 2 * SPAN), lambda i, *_: (0, 0, 0)),
                pl.BlockSpec((fields, pairs, 2, width), lambda i, *_: (0, 0, 0, 0)),
                pl.BlockSpec((pairs // 2, 128), lambda i, *_: (0, 0)),
            ],
            scratch_shapes=[pltpu.VMEM((2, HALF // 8, LANES), F32), pltpu.VMEM((64 * pairs + 16, 128), F32)],
        ),
        out_shape=[
            jax.ShapeDtypeStruct((cycles, 4 * HALF, 256), BF16),
            jax.ShapeDtypeStruct((cycles, 4, 16, 2 * HALF), F32),
            jax.ShapeDtypeStruct((2, 64 * pairs, 2 * SPAN), BF16),
            jax.ShapeDtypeStruct(spectral_in.shape, BF16),
            jax.ShapeDtypeStruct((pairs // 2, 128), jnp.int32),
        ],
        compiler_params=params(53.3),
        cost_estimate=pl.CostEstimate(flops=20_000_000, bytes_accessed=16_000_000, transcendentals=0),
    )(cycle_points, assignment.reshape(pairs // 2, 128), spectral_in)

    shift = [[(i, (i + k) % 4) for i in range(4)] for k in range(4)]
    gathered = [own] + [lax.ppermute(spectral_in, "lev", shift[k]) for k in range(1, 4)]

    sent = pl.pallas_call(
        functools.partial(legendre_kernel, pairs, cycles, slots),
        grid_spec=pltpu.PrefetchScalarGridSpec(
            num_scalar_prefetch=1,
            grid=(pairs,),
            in_specs=[
                pl.BlockSpec(memory_space=pltpu.HBM),
                ] + [pl.BlockSpec((fields, pairs, 2, width), lambda i, *_: (0, 0, 0, 0))] * 4,
            out_specs=pl.BlockSpec((64, slots // 2, 2, 128), lambda i, *_: (0, 0, 0, 0)),
            scratch_shapes=[
                pltpu.VMEM((64 * slots + 56, 128), F32),
                pltpu.VMEM((32, width), F32),
                pltpu.VMEM((pairs, quarter, width), BF16),
                pltpu.SemaphoreType.DMA((pairs,)),
            ],
        ),
        out_shape=jax.ShapeDtypeStruct((64, slots // 2, 2, 128), BF16),
        compiler_params=params(52),
        cost_estimate=pl.CostEstimate(flops=1_100_000_000, bytes_accessed=11_000_000, transcendentals=0),
    )(held, legendre, *gathered)

    received = lax.all_to_all(sent, "lat", split_axis=0, concat_axis=0, tiled=True)

    returned = pl.pallas_call(
        functools.partial(grid_kernel, cycles, pairs, slots, back_slots),
        grid_spec=pltpu.PrefetchScalarGridSpec(
            num_scalar_prefetch=1,
            grid=(cycles,),
            in_specs=[
                pl.BlockSpec((64, slots // 2, 2, 128), lambda i, *_: (0, 0, 0, 0)),
                pl.BlockSpec(memory_space=pltpu.HBM),
                pl.BlockSpec(memory_space=pltpu.HBM),
                pl.BlockSpec(memory_space=pltpu.HBM),
            ],
            out_specs=pl.BlockSpec((64, back_slots // 2, 2, 128), lambda i, *_: (0, 0, 0, 0)),
            scratch_shapes=[
                pltpu.VMEM((64 * slots + 56, 128), F32),
                pltpu.VMEM((64 * pairs, 128), F32),
                pltpu.VMEM((2, 64 * cycles, 64 * pairs), BF16),
                pltpu.VMEM((64 * cycles, 2 * HALF), F32),
                pltpu.VMEM((2, 32 * ROWS, 2 * HALF), BF16),
                pltpu.VMEM((32 * ROWS, 512), F32),
                pltpu.VMEM((16 * ROWS, 512), BF16),
                pltpu.VMEM((10 * 32 * cycles + 8, 128), F32),
                pltpu.VMEM((64 * back_slots + 32, 128), F32),
                pltpu.VMEM((2, 64 * pairs, 2 * SPAN), BF16),
                pltpu.VMEM((cycles, 4 * HALF, 256), BF16),
                pltpu.VMEM((cycles, 4, 16, 2 * HALF), F32),
                pltpu.SemaphoreType.DMA((2 * cycles + 1,)),
            ],
        ),
        out_shape=jax.ShapeDtypeStruct((64, back_slots // 2, 2, 128), BF16),
        compiler_params=params(53),
        cost_estimate=pl.CostEstimate(flops=5_000_000_000, bytes_accessed=13_000_000, transcendentals=0),
    )(cycle_points, received, place, tables, rows)

    home = lax.all_to_all(returned, "lat", split_axis=0, concat_axis=0, tiled=True)

    parts = []
    for first in range(0, pairs, pairs // 2):
        half = pairs // 2
        blocks = pl.pallas_call(
            functools.partial(inverse_kernel, pairs, first, back_slots),
            grid_spec=pltpu.PrefetchScalarGridSpec(
                num_scalar_prefetch=1,
                grid=(half,),
                in_specs=[
                    pl.BlockSpec((64, back_slots // 2, 2, 128), lambda i, *_: (0, 0, 0, 0)),
                    pl.BlockSpec(memory_space=pltpu.HBM),
                    pl.BlockSpec((1, quarter), lambda i, *_: (0, 0)),
                ],
                out_specs=[pl.BlockSpec((2, half, 2, width), lambda i, *_: (0, 0, 0, 0))] * 4,
                scratch_shapes=[
                    pltpu.VMEM((64 * back_slots + 32, 128), F32),
                    pltpu.VMEM((half, quarter, width), BF16),
                    pltpu.SemaphoreType.DMA((half,)),
                ],
            ),
            out_shape=[jax.ShapeDtypeStruct((2, half, 2, width), BF16)] * 4,
            compiler_params=params(52),
            cost_estimate=pl.CostEstimate(flops=300_000_000, bytes_accessed=5_000_000, transcendentals=0),
        )(assignment, home, legendre, weights.reshape(1, quarter))
        total = blocks[0].astype(F32)
        for k in range(1, 4):
            came = lax.ppermute(blocks[k], "lev", [(i, (i - k) % 4) for i in range(4)])
            total = total + came.astype(F32)
        parts.append(total)
    return jnp.concatenate(parts, axis=1) * (math.sqrt(width - 1) / 2.0)


def solution(mesh):
    return jax.shard_map(
        on_device,
        mesh=mesh,
        in_specs=(P("lev", "lat", None, None), P("lat", "lev", None), P("lev"), P(), P()),
        out_specs=P("lev", "lat", None, None),
        check_vma=False,
    )
```

```python
import functools
import math

import jax
import jax.numpy as jnp
from jax import lax
from jax.experimental import pallas as pl
from jax.experimental.pallas import tpu as pltpu
from jax.sharding import PartitionSpec as P

F32 = jnp.float32
BF16 = jnp.bfloat16

LANES = 128
ROWS = 11
HALF = 640
AHEAD = 3
SPAN = 384


def turn(frac):
    x = frac * math.pi
    y = x * x
    s = F32(-1.0 / 39916800.0)
    for c in (1.0 / 362880.0, -1.0 / 5040.0, 1.0 / 120.0, -1.0 / 6.0, 1.0):
        s = s * y + F32(c)
    s = s * x
    c2 = F32(1.0 / 479001600.0)
    for c in (-1.0 / 3628800.0, 1.0 / 40320.0, -1.0 / 720.0, 1.0 / 24.0, -0.5, 1.0):
        c2 = c2 * y + F32(c)
    return 1.0 - 2.0 * s * s, 2.0 * s * c2


def angle(product, length, inverse):
    whole = jnp.floor(product * inverse)
    frac = (product - whole * length) * inverse
    return frac - jnp.where(frac > 0.5, F32(1.0), F32(0.0))


def cycle_length(points_ref, cycles, step):
    return points_ref[lax.axis_index("lev") * (64 * cycles) + 64 * step + lax.axis_index("lat")]


def table_kernel(cycles, pairs, points_ref, asg_ref, spec_ref, t_ref, a_ref, p_ref, own_ref, asg_out, r_scr, col_scr):
    step = pl.program_id(0)
    length_i = cycle_length(points_ref, cycles, step)
    length = length_i.astype(F32)
    inverse = 1.0 / jnp.full((1, 1), length, F32)

    @pl.when(step == 0)
    def _():
        own_ref[...] = spec_ref[...]
        asg_out[...] = asg_ref[...]
        for k in range(pairs // 2):
            row = asg_ref[k : k + 1, :].astype(F32)
            col_scr[128 * k : 128 * k + 128, :] = jnp.broadcast_to(row, (128, 128)).T
        lane = lax.broadcasted_iota(jnp.int32, (1, 128), 1).astype(F32)
        for p in range(pairs):
            pair = col_scr[pl.ds(p, 64, stride=pairs), :]
            for t in range(2):
                for k in range(SPAN // 128):
                    low = 2.0 * (lane + 128.0 * k) + float(t)
                    high = 1279.0 - 2.0 * (lane + float(HALF - SPAN + 128 * k)) - float(t)
                    rows = slice(64 * p, 64 * p + 64)
                    cols = slice(SPAN * t + 128 * k, SPAN * t + 128 * k + 128)
                    p_ref[0, rows, cols] = jnp.where(pair == low, F32(1), F32(0)).astype(BF16)
                    p_ref[1, rows, cols] = jnp.where(pair == high, F32(1), F32(0)).astype(BF16)

    r = lax.broadcasted_iota(jnp.int32, (HALF // 8, LANES), 1).astype(F32)
    u1 = lax.broadcasted_iota(jnp.int32, (HALF // 8, LANES), 0).astype(F32)
    rc, rs = turn(angle(16.0 * u1 * r, length, inverse))
    r_scr[0] = rc
    r_scr[1] = rs
    u2 = lax.broadcasted_iota(jnp.int32, (8, LANES), 0)
    r8 = lax.broadcasted_iota(jnp.int32, (8, LANES), 1).astype(F32)
    flip8 = jnp.where((u2 & 1) == 1, F32(-1), F32(1))
    flip = jnp.concatenate([flip8, flip8], axis=0)
    for t in range(2):
        vc, vs = turn(angle((2.0 * u2.astype(F32) + float(t)) * r8, length, inverse))
        for k in range(HALF // 16):
            parts = []
            for e in range(2):
                w = 2 * k + e
                bc = r_scr[0, w : w + 1, :]
                bs = r_scr[1, w : w + 1, :]
                parts.append((bc * vc - bs * vs, bc * vs + bs * vc))
            cc = jnp.concatenate([parts[0][0], parts[1][0]], axis=0)
            ss = jnp.concatenate([parts[0][1], parts[1][1]], axis=0)
            top = 2 * HALF * t + 16 * k
            low = top + HALF
            t_ref[0, top : top + 16, :LANES] = cc.astype(BF16)
            t_ref[0, low : low + 16, :LANES] = (-ss).astype(BF16)
            if t == 0:
                t_ref[0, top : top + 16, LANES:] = (flip * cc).astype(BF16)
                t_ref[0, low : low + 16, LANES:] = (-flip * ss).astype(BF16)
            else:
                t_ref[0, top : top + 16, LANES:] = (flip * ss).astype(BF16)
                t_ref[0, low : low + 16, LANES:] = (flip * cc).astype(BF16)

    limit = jnp.minimum((length_i - 1) // 2, 1279)
    for t in range(2):
        m = 2 * lax.broadcasted_iota(jnp.int32, (16, HALF), 1) + t
        q = lax.broadcasted_iota(jnp.int32, (16, HALF), 0)
        ac, as_ = turn(angle((m * (LANES * q)).astype(F32), length, inverse))
        keep = m <= limit
        up = jnp.where(keep, jnp.where(m == 0, F32(1), F32(2)), F32(0))
        down = jnp.where(keep, jnp.broadcast_to(inverse, m.shape), F32(0))
        lanes = slice(HALF * t, HALF * t + HALF)
        a_ref[0, 0, :, lanes] = up * ac
        a_ref[0, 1, :, lanes] = up * as_
        a_ref[0, 2, :, lanes] = down * ac
        a_ref[0, 3, :, lanes] = down * as_


def legendre_kernel(pairs, cycles, slots, asg_ref, leg_hbm, *rest):
    specs, (out_ref, scr, xs, leg_all, sems) = rest[:4], rest[4:]
    p = pl.program_id(0)

    def fetch(k):
        return pltpu.make_async_copy(leg_hbm.at[k], leg_all.at[k], sems.at[k])

    @pl.when(p == 0)
    def _():
        for k in range(AHEAD):
            fetch(k).start()

    @pl.when(p + AHEAD < pairs)
    def _():
        fetch(p + AHEAD).start()

    place = lax.axis_index("lat") * pairs + p
    split = 1280 - asg_ref[place // 128, place % 128]
    column = lax.broadcasted_iota(jnp.int32, (1, 1281), 1)
    second = column >= split
    odd = (jnp.where(second, column - split, column) & 1) == 1
    first_f = jnp.where(second, F32(0), F32(1))
    second_f = jnp.where(second, F32(1), F32(0))
    sign = jnp.where(odd, F32(-1), F32(1))
    for f in range(16):
        o, e = f // 2, f % 2
        pair = specs[f // 4][f % 4, p].astype(F32)
        xs[8 * e + o : 8 * e + o + 1, :] = pair[:1]
        xs[16 + 8 * e + o : 17 + 8 * e + o, :] = pair[1:]
    spec = xs[...]
    blocks = []
    for seg in (first_f, second_f):
        for i in range(2):
            for e in range(2):
                rows = spec[16 * i + 8 * e : 16 * i + 8 * e + 8]
                blocks.append(rows * seg)
                blocks.append(rows * (seg * sign))
    x = jnp.concatenate(blocks, axis=0)
    last = jnp.broadcast_to(x[:, 1280:], (128, 128)).T[:1]
    x = x[:, :1280].astype(BF16)
    fetch(p).wait()
    y = lax.dot_general(leg_all[p, :, :1280], x, (((1,), (1,)), ((), ())), preferred_element_type=F32)
    y = y + leg_all[p, :, 1280:].astype(F32) * last

    for jj in range(cycles):
        scr[pl.ds(p * cycles + jj, 64, stride=slots), :] = y[64 * jj : 64 * jj + 64]

    @pl.when(p == pairs - 1)
    def _():
        out_ref[...] = scr[: 64 * slots].reshape(out_ref.shape).astype(BF16)


def grid_kernel(cycles, pairs, slots, back_slots, points_ref, r_ref, p_hbm, t_hbm, a_hbm, out_ref,
                xf, xs, xt, y, m, g, hb, o, pf, p_ref, t_all, a_all, sems):
    step = pl.program_id(0)

    def table_copies(k):
        return (
            pltpu.make_async_copy(t_hbm.at[k], t_all.at[k], sems.at[k]),
            pltpu.make_async_copy(a_hbm.at[k], a_all.at[k], sems.at[cycles + k]),
        )

    place_copy = pltpu.make_async_copy(p_hbm, p_ref, sems.at[2 * cycles])

    @pl.when(step == 0)
    def _():
        place_copy.start()
        for copy in table_copies(0):
            copy.start()
        xf[: 64 * slots] = r_ref[...].astype(F32).reshape(64 * slots, 128)
        for jj in range(cycles):
            for p in range(pairs):
                xs[64 * p : 64 * p + 64, :] = xf[pl.ds(p * cycles + jj, 64, stride=slots), :]
            turned = xs[...].T.astype(BF16)
            xt[0, 64 * jj : 64 * jj + 64, :] = turned[:64]
            xt[1, 64 * jj : 64 * jj + 64, :] = turned[64:]
        place_copy.wait()
        for t in range(2):
            cols = slice(SPAN * t, SPAN * t + SPAN)
            y0 = jnp.dot(xt[0], p_ref[0, :, cols], preferred_element_type=F32)
            y1 = jnp.dot(xt[1], p_ref[1, :, cols], preferred_element_type=F32)
            y[:, HALF * t : HALF * t + 256] = y0[:, :256]
            y[:, HALF * t + 256 : HALF * t + 384] = y0[:, 256:] + y1[:, :128]
            y[:, HALF * t + 384 : HALF * t + 640] = y1[:, 128:]

    @pl.when(step + 1 < cycles)
    def _():
        for copy in table_copies(step + 1):
            copy.start()

    for copy in table_copies(step):
        copy.wait()
    t_ref, a_ref = t_all.at[step], a_all.at[step]
    base = pl.multiple_of(step * 64, 64)
    for t in range(2):
        lanes = slice(HALF * t, HALF * t + HALF)
        fr = y[pl.ds(base, 32), lanes]
        fi = y[pl.ds(base + 32, 32), lanes]
        for q in range(ROWS):
            ar = a_ref[0, q : q + 1, lanes]
            ai = a_ref[1, q : q + 1, lanes]
            m[t, 32 * q : 32 * q + 32, :HALF] = (fr * ar - fi * ai).astype(BF16)
            m[t, 32 * q : 32 * q + 32, HALF:] = (fr * ai + fi * ar).astype(BF16)
        g[:, 256 * t : 256 * t + 256] = jnp.dot(
            m[t], t_ref[2 * HALF * t : 2 * HALF * t + 2 * HALF, :], preferred_element_type=F32
        )

    quarter = cycle_length(points_ref, cycles, step) // 4
    lane = lax.broadcasted_iota(jnp.int32, (16, LANES), 1)
    for q in range(ROWS):
        rows = slice(32 * q, 32 * q + 32)
        even, turned = g[rows, 0:128], g[rows, 128:256]
        odd, skew = g[rows, 256:384], g[rows, 384:512]
        inside = lane < quarter - LANES * q
        flux = []
        for value in (even + odd, turned - skew, even - odd, turned + skew):
            flux.append(jnp.where(inside, value[:16] * value[16:], F32(0)))
        f0, f1, f2, f3 = flux
        back_rows = slice(16 * q, 16 * q + 16)
        hb[back_rows, 0:128] = (f0 + f2).astype(BF16)
        hb[back_rows, 128:256] = (f1 + f3).astype(BF16)
        hb[back_rows, 256:384] = (f0 - f2).astype(BF16)
        hb[back_rows, 384:512] = (f3 - f1).astype(BF16)

    out_base = pl.multiple_of(step * 32, 32)
    for t in range(2):
        lanes = slice(HALF * t, HALF * t + HALF)
        b = lax.dot_general(hb[:, 256 * t : 256 * t + 256], t_ref[2 * HALF * t : 2 * HALF * t + 2 * HALF, :],
                            (((1,), (1,)), ((), ())), preferred_element_type=F32)
        real = jnp.zeros((16, HALF), F32)
        imag = jnp.zeros((16, HALF), F32)
        for q in range(ROWS):
            br = b[16 * q : 16 * q + 16, :HALF]
            bi = b[16 * q : 16 * q + 16, HALF:]
            ar = a_ref[2, q : q + 1, lanes]
            ai = a_ref[3, q : q + 1, lanes]
            real = real + (ar * br + ai * bi)
            imag = imag + (ar * bi - ai * br)
        for k in range(HALF // 128):
            sub = slice(128 * k, 128 * k + 128)
            tile = (5 * t + k) * 32 * cycles
            o[pl.ds(tile + out_base, 16, stride=2), :] = real[:, sub]
            o[pl.ds(tile + out_base + 1, 16, stride=2), :] = imag[:, sub]

    @pl.when(step == cycles - 1)
    def _():
        tails = []
        size = 32 * cycles
        for s in range(2):
            total = None
            for t in range(2):
                tile = (5 * t + 2 * s) * size
                piece = jnp.concatenate(
                    [o[tile + size * k : tile + size * k + size, :] for k in range(3)], axis=1
                ).astype(BF16)
                part = lax.dot_general(p_ref[s, :, SPAN * t : SPAN * t + SPAN], piece,
                                       (((1,), (1,)), ((), ())), preferred_element_type=F32)
                total = part if total is None else total + part
            for p in range(pairs):
                pf[pl.ds(2 * p + s, 64, stride=back_slots), :] = total[64 * p : 64 * p + 64, :128]
            tails.append(total[:, 128:])
        both = jnp.concatenate(tails, axis=1)
        for k in range(pairs // 2):
            pf[pl.ds(2 * pairs + k, 64, stride=back_slots), :] = jnp.concatenate(
                [both[128 * k : 128 * k + 64], both[128 * k + 64 : 128 * k + 128]], axis=1
            )
        if back_slots > 5 * pairs // 2:
            pf[pl.ds(back_slots - 1, 64, stride=back_slots), :] = jnp.zeros((64, 128), F32)
        out_ref[...] = pf[: 64 * back_slots].reshape(out_ref.shape).astype(BF16)


def inverse_kernel(pairs, first, back_slots, asg_ref, r_ref, leg_hbm, w_ref, *rest):
    outs, (rf, leg_all, sems) = rest[:4], rest[4:]
    step = pl.program_id(0)
    p = step + first

    def fetch(k):
        return pltpu.make_async_copy(leg_hbm.at[first + k], leg_all.at[k], sems.at[k])

    @pl.when(step == 0)
    def _():
        for k in range(AHEAD):
            fetch(k).start()
        rf[: 64 * back_slots] = r_ref[...].astype(F32).reshape(64 * back_slots, 128)

    @pl.when(step + AHEAD < pairs)
    def _():
        fetch(step + AHEAD).start()

    weight = w_ref[...]
    blocks = []
    for b in (2 * p, 2 * p + 1, 2 * pairs + p // 2):
        blocks.append(rf[pl.ds(b, 64, stride=back_slots), :])
    z = jnp.concatenate(blocks + [jnp.zeros_like(blocks[0])], axis=0).T
    late = jnp.where(p % 2 == 0, z[:64, 128:192], z[64:, 128:192])
    left = []
    for s in range(2):
        cols = [z[32 * jj : 32 * jj + 32, 64 * s : 64 * s + 64] for jj in range(4)]
        cols.append(late[32 * s : 32 * s + 32])
        zs = jnp.concatenate(cols, axis=1)
        north, south = zs[:16], zs[16:]
        left.append(weight * (north + south))
        left.append(weight * (north - south))
    lhs = jnp.concatenate(left, axis=0).astype(BF16)
    fetch(step).wait()
    res = jnp.dot(lhs, leg_all[step], preferred_element_type=F32)
    split = 1280 - asg_ref[lax.axis_index("lat") * pairs + p]
    column = lax.broadcasted_iota(jnp.int32, (1, 1281), 1)
    second = column >= split
    odd = (jnp.where(second, column - split, column) & 1) == 1
    value = jnp.where(
        second,
        jnp.where(odd, res[48:64], res[32:48]),
        jnp.where(odd, res[16:32], res[0:16]),
    )
    for k in range(4):
        rows = value[4 * k : 4 * k + 4].astype(BF16)
        outs[k][0, step] = rows[:2]
        outs[k][1, step] = rows[2:]


def params(mib):
    return pltpu.CompilerParams(vmem_limit_bytes=int(mib * 1024 * 1024))


def on_device(spectral_in, legendre, weights, cycle_points, assignment):
    pairs, quarter, width = legendre.shape
    cycles = quarter // 64
    slots = 50
    back_slots = 26
    fields = spectral_in.shape[0]

    tables, rows, place, own, held = pl.pallas_call(
        functools.partial(table_kernel, cycles, pairs),
        grid_spec=pltpu.PrefetchScalarGridSpec(
            num_scalar_prefetch=1,
            grid=(cycles,),
            in_specs=[
                pl.BlockSpec((pairs // 2, 128), lambda i, *_: (0, 0)),
                pl.BlockSpec((fields, pairs, 2, width), lambda i, *_: (0, 0, 0, 0)),
            ],
            out_specs=[
                pl.BlockSpec((1, 4 * HALF, 256), lambda i, *_: (i, 0, 0)),
                pl.BlockSpec((1, 4, 16, 2 * HALF), lambda i, *_: (i, 0, 0, 0)),
                pl.BlockSpec((2, 64 * pairs, 2 * SPAN), lambda i, *_: (0, 0, 0)),
                pl.BlockSpec((fields, pairs, 2, width), lambda i, *_: (0, 0, 0, 0)),
                pl.BlockSpec((pairs // 2, 128), lambda i, *_: (0, 0)),
            ],
            scratch_shapes=[pltpu.VMEM((2, HALF // 8, LANES), F32), pltpu.VMEM((64 * pairs + 16, 128), F32)],
        ),
        out_shape=[
            jax.ShapeDtypeStruct((cycles, 4 * HALF, 256), BF16),
            jax.ShapeDtypeStruct((cycles, 4, 16, 2 * HALF), F32),
            jax.ShapeDtypeStruct((2, 64 * pairs, 2 * SPAN), BF16),
            jax.ShapeDtypeStruct(spectral_in.shape, BF16),
            jax.ShapeDtypeStruct((pairs // 2, 128), jnp.int32),
        ],
        compiler_params=params(53.3),
        cost_estimate=pl.CostEstimate(flops=20_000_000, bytes_accessed=16_000_000, transcendentals=0),
    )(cycle_points, assignment.reshape(pairs // 2, 128), spectral_in)

    shift = [[(i, (i + k) % 4) for i in range(4)] for k in range(4)]
    gathered = [own] + [lax.ppermute(spectral_in, "lev", shift[k]) for k in range(1, 4)]

    sent = pl.pallas_call(
        functools.partial(legendre_kernel, pairs, cycles, slots),
        grid_spec=pltpu.PrefetchScalarGridSpec(
            num_scalar_prefetch=1,
            grid=(pairs,),
            in_specs=[
                pl.BlockSpec(memory_space=pltpu.HBM),
                ] + [pl.BlockSpec((fields, pairs, 2, width), lambda i, *_: (0, 0, 0, 0))] * 4,
            out_specs=pl.BlockSpec((64, slots // 2, 2, 128), lambda i, *_: (0, 0, 0, 0)),
            scratch_shapes=[
                pltpu.VMEM((64 * slots + 56, 128), F32),
                pltpu.VMEM((32, width), F32),
                pltpu.VMEM((pairs, quarter, width), BF16),
                pltpu.SemaphoreType.DMA((pairs,)),
            ],
        ),
        out_shape=jax.ShapeDtypeStruct((64, slots // 2, 2, 128), BF16),
        compiler_params=params(52),
        cost_estimate=pl.CostEstimate(flops=1_100_000_000, bytes_accessed=11_000_000, transcendentals=0),
    )(held, legendre, *gathered)

    received = lax.all_to_all(sent, "lat", split_axis=0, concat_axis=0, tiled=True)

    returned = pl.pallas_call(
        functools.partial(grid_kernel, cycles, pairs, slots, back_slots),
        grid_spec=pltpu.PrefetchScalarGridSpec(
            num_scalar_prefetch=1,
            grid=(cycles,),
            in_specs=[
                pl.BlockSpec((64, slots // 2, 2, 128), lambda i, *_: (0, 0, 0, 0)),
                pl.BlockSpec(memory_space=pltpu.HBM),
                pl.BlockSpec(memory_space=pltpu.HBM),
                pl.BlockSpec(memory_space=pltpu.HBM),
            ],
            out_specs=pl.BlockSpec((64, back_slots // 2, 2, 128), lambda i, *_: (0, 0, 0, 0)),
            scratch_shapes=[
                pltpu.VMEM((64 * slots + 56, 128), F32),
                pltpu.VMEM((64 * pairs, 128), F32),
                pltpu.VMEM((2, 64 * cycles, 64 * pairs), BF16),
                pltpu.VMEM((64 * cycles, 2 * HALF), F32),
                pltpu.VMEM((2, 32 * ROWS, 2 * HALF), BF16),
                pltpu.VMEM((32 * ROWS, 512), F32),
                pltpu.VMEM((16 * ROWS, 512), BF16),
                pltpu.VMEM((10 * 32 * cycles + 8, 128), F32),
                pltpu.VMEM((64 * back_slots + 32, 128), F32),
                pltpu.VMEM((2, 64 * pairs, 2 * SPAN), BF16),
                pltpu.VMEM((cycles, 4 * HALF, 256), BF16),
                pltpu.VMEM((cycles, 4, 16, 2 * HALF), F32),
                pltpu.SemaphoreType.DMA((2 * cycles + 1,)),
            ],
        ),
        out_shape=jax.ShapeDtypeStruct((64, back_slots // 2, 2, 128), BF16),
        compiler_params=params(53),
        cost_estimate=pl.CostEstimate(flops=5_000_000_000, bytes_accessed=13_000_000, transcendentals=0),
    )(cycle_points, received, place, tables, rows)

    home = lax.all_to_all(returned, "lat", split_axis=0, concat_axis=0, tiled=True)

    blocks = pl.pallas_call(
        functools.partial(inverse_kernel, pairs, 0, back_slots),
        grid_spec=pltpu.PrefetchScalarGridSpec(
            num_scalar_prefetch=1,
            grid=(pairs,),
            in_specs=[
                pl.BlockSpec((64, back_slots // 2, 2, 128), lambda i, *_: (0, 0, 0, 0)),
                pl.BlockSpec(memory_space=pltpu.HBM),
                pl.BlockSpec((1, quarter), lambda i, *_: (0, 0)),
            ],
            out_specs=[pl.BlockSpec((2, pairs, 2, width), lambda i, *_: (0, 0, 0, 0))] * 4,
            scratch_shapes=[
                pltpu.VMEM((64 * back_slots + 32, 128), F32),
                pltpu.VMEM((pairs, quarter, width), BF16),
                pltpu.SemaphoreType.DMA((pairs,)),
            ],
        ),
        out_shape=[jax.ShapeDtypeStruct((2, pairs, 2, width), BF16)] * 4,
        compiler_params=params(52),
        cost_estimate=pl.CostEstimate(flops=600_000_000, bytes_accessed=10_000_000, transcendentals=0),
    )(assignment, home, legendre, weights.reshape(1, quarter))
    total = blocks[0].astype(F32)
    for k in range(1, 4):
        came = lax.ppermute(blocks[k], "lev", [(i, (i - k) % 4) for i in range(4)])
        total = total + came.astype(F32)
    return total * (math.sqrt(width - 1) / 2.0)


def solution(mesh):
    return jax.shard_map(
        on_device,
        mesh=mesh,
        in_specs=(P("lev", "lat", None, None), P("lat", "lev", None), P("lev"), P(), P()),
        out_specs=P("lev", "lat", None, None),
        check_vma=False,
    )
```
